512 devices in a mesh: section: 16 (over y, x), expert: 32 (over z, core).
Axes of the slice: x: 4, y: 4, z: 16, core: 2. Of those that a mesh axis runs over, the one named last changes fastest.
Arguments:
- activations: bfloat16 [2, 32768, 4096], P(None, ('section', 'expert')), may hold values from -6 to 6
- expert_ids: int32 [2, 2, 32768, 8], P(None, None, ('section', 'expert')), may hold values from 0 to 127, all different within a row; in each aligned block of 64 rows (0 to 63, 64 to 127, ..., all dimensions but the last counted through in order) at most 6 rows name the same one
- gate_values: float32 [2, 2, 32768, 8], P(None, None, ('section', 'expert')), may hold values from 0.1 to 1
- w_gate: bfloat16 [16, 4096, 4096], P('section', None, 'expert'), may hold values from -0.09375 to 0.09375
- w_up: bfloat16 [16, 4096, 4096], P('section', None, 'expert'), may hold values from -0.09375 to 0.09375
- w_down: bfloat16 [16, 4096, 4096], P('section', 'expert'), may hold values from -0.75 to 0.75
Outputs:
- carried: bfloat16 [2, 32768, 4096], P(None, ('section', 'expert'))
The draws below stay inside these ranges and needn't reach their ends.
Inputs may be any that keep to these rules, and one draw needn't show every extreme that they name: `expert_ids`: each token's 8 ids are different experts. In each aligned block of 64 rows (one device's tokens of one direction at one step) no expert is named by more than 6 rows, a bound that some block reaches.
All inputs are finite; a program needn't handle non-finite values.
Results may differ from the reference program's by a relative error of at most 0.012.
Values may be sent and summed in bfloat16 or wider, within the bound.
No kernel may reach another device: no remote copies, remote signals or barrier semaphores. Data moves between devices by JAX's collectives and lax.ppermute only.
A program may use at most 64 MiB of HBM per device.

```python
import math
import jax
import jax.numpy as jnp
import numpy as np
from jax import lax

D = 4096
EXPERTS = 128
TOPK = 8
HE = 1024
HS = 128
ROWS = 64
MOST = 6
STEPS = 2
EXP_WIN = 4
ALL = 32768
N_SECTION = 16
N_EXPERT = 32


def levels(stream_key, dims, cuts, smallest, largest):
    def one(position, blocks):
        heights = jax.random.uniform(jax.random.fold_in(jax.random.fold_in(stream_key, 6), position), (blocks,), jnp.float32, smallest / len(cuts), largest / len(cuts))
        return jnp.repeat(jnp.exp(heights), dims[position] // blocks).reshape((-1,) + (1,) * (len(dims) - position - 1))

    loudness = one(*cuts[0])
    for cut in cuts[1:]:
        loudness = loudness * one(*cut)
    return loudness


def deal_out(key, own, number, rows, count, top, bound, lean):
    sequence = jax.random.permutation(key, count)
    packed, ordinary = load_shares(count, rows * top, bound, lean, True), load_shares(count, rows * top, bound, lean, False)
    places = jnp.arange(count)

    def named(lengths, offset_by):
        used = int((lengths > 0).sum())
        fixed = max(1, used // 4)
        moved = fixed + (places - fixed + offset_by * (used - fixed)) % max(1, count - fixed)
        return jnp.zeros((count,), jnp.int32).at[sequence[jnp.where(places < fixed, places, moved)]].set(jnp.asarray(lengths, jnp.int32))

    lengths = jnp.where(number % 4 == 0, named(packed, number // 4), named(ordinary, number - number // 4 - 1))
    mixed = jax.random.permutation(jax.random.fold_in(own, 3), count)
    donor, receiver = mixed[0:count // 2 * 2:2], mixed[1:count // 2 * 2:2]
    slack = jnp.minimum(lengths[donor] - 1, bound - lengths[receiver]) // 2
    slack = jnp.where((donor == sequence[0]) | (receiver == sequence[0]) | (lengths[receiver] == 0), 0, jnp.maximum(slack, 0))
    moved = jax.random.randint(jax.random.fold_in(own, 4), (count // 2,), 0, 1 << 20) % (slack + 1)
    lengths = lengths.at[donor].add(-moved).at[receiver].add(moved)
    labels = jnp.searchsorted(jnp.cumsum(lengths), jnp.arange(rows * top), side="right").astype(jnp.int32)
    listing = labels.reshape(top, rows).T
    listing = listing[jax.random.permutation(jax.random.fold_in(own, 1), rows)]
    offset_by = jax.random.randint(jax.random.fold_in(own, 2), (rows, 1), 0, top)
    return jnp.take_along_axis(listing, (jnp.arange(top)[None, :] + offset_by) % top, axis=1)


def load_shares(number_of, total, reach, lean, full):
    loads = [(1 << 20) // math.isqrt(standing ** lean) + 1 for standing in range(1, number_of + 1)]
    largest = reach if full else min(reach, max(-(-total // number_of), total * loads[0] // sum(loads)))
    least = 1 if total - largest >= number_of - 1 else 0
    given, surplus = [largest] + [least] * (number_of - 1), total - largest - least * (number_of - 1)
    while surplus > 0:
        candidates = [i for i in range(1, number_of) if given[i] < largest] or [i for i in range(1, number_of) if given[i] < reach]
        whole, left = sum([loads[i] for i in candidates]), surplus
        for i in candidates:
            addition = min(reach - given[i], max(1, left * loads[i] // whole), surplus)
            given[i] = given[i] + addition
            surplus = surplus - addition
    return np.array(given)


def scatter_about(stream_key, shape, deviation, reach, cuts=(), held_as=jnp.bfloat16):
    entries = jax.random.normal(stream_key, shape, jnp.float32) * deviation
    if len(cuts) > 0:
        entries = levels(stream_key, shape, cuts, -0.22, 0.18) * entries
    return jnp.clip(entries, min=-reach, max=reach).astype(held_as)


def setup_inputs(seed: int = 0) -> dict:
    seeds = jax.random.split(jax.random.key(seed), 7)
    activations = scatter_about(seeds[0], (2, ALL, D), 1.0, 6.0, ((1, 512),))
    expert_ids_keys = jax.random.split(jax.random.fold_in(seeds[1], 1), STEPS * 2 * ALL // ROWS)
    expert_ids_turns = jax.random.permutation(jax.random.fold_in(seeds[1], 3), STEPS * 2 * ALL // ROWS)
    expert_ids = jax.vmap(lambda own, number: deal_out(jax.random.fold_in(seeds[1], 2), own, number, ROWS, EXPERTS, TOPK, MOST, 2))(expert_ids_keys, expert_ids_turns).reshape((STEPS, 2, ALL, TOPK))
    gate_values = jnp.clip(jnp.exp(math.log(1.0) - 2.3025851 * jax.random.uniform(seeds[2], (STEPS, 2, ALL, TOPK), jnp.float32) ** levels(seeds[2], (STEPS, 2, ALL, TOPK), ((2, 512),), -0.2, 0.2)), 0.1, 1.0)
    w_gate = scatter_about(seeds[3], (N_SECTION, D, EXP_WIN * HE), D ** -0.5, 0.09375, ((0, 16), (2, 32)))
    w_up = scatter_about(seeds[4], (N_SECTION, D, EXP_WIN * HE), D ** -0.5, 0.09375, ((0, 16), (2, 32)))
    w_down = scatter_about(seeds[5], (N_SECTION, EXP_WIN * HE, D), (HE // 16) ** -0.5, 0.75, ((0, 16), (1, 32)))
    return dict(activations=activations, expert_ids=expert_ids, gate_values=gate_values, w_gate=w_gate, w_up=w_up, w_down=w_down)


def route_tables(ids, gates, expert_window, most):
    norm = gates / jnp.sum(gates, axis=-1, keepdims=True)
    picks = ids[..., None] == jnp.arange(expert_window, dtype=jnp.int32)
    member = jnp.any(picks, axis=-2).astype(jnp.int32)
    weight_matrix = jnp.sum(jnp.where(picks, norm[..., None], 0.0), axis=-2)
    rank = jnp.cumsum(member, axis=-2) - member
    placement_slot = (rank[..., None] == jnp.arange(most, dtype=jnp.int32)) & (member[..., None] > 0)
    return placement_slot.astype(jnp.float32), weight_matrix


def reference(activations, expert_ids, gate_values, w_gate, w_up, w_down):
    split = HE // HS
    expert_window = N_EXPERT * HS // HE
    carry_state = activations.reshape(2, N_SECTION, N_EXPERT, ROWS, D)
    for step in range(STEPS):
        ids = expert_ids[step].reshape(2, N_SECTION, N_EXPERT, ROWS, TOPK)
        gates = gate_values[step].reshape(2, N_SECTION, N_EXPERT, ROWS, TOPK)

        def one_section(pack):
            block, idv, gatev, wg, wu, wd = pack
            placement_slot, weight_matrix = route_tables(idv, gatev, expert_window, MOST)
            listed = jnp.einsum("dnrem,dnrf->ednmf", placement_slot, block.astype(jnp.float32), precision=lax.Precision.HIGHEST).astype(jnp.bfloat16)
            output_rows = []
            for expert in range(expert_window):
                lower = expert * HE
                rows_e = listed[expert].reshape(-1, D)
                gate_part = jnp.dot(rows_e, wg[:, lower:lower + HE], preferred_element_type=jnp.float32)
                up_projection = jnp.dot(rows_e, wu[:, lower:lower + HE], preferred_element_type=jnp.float32)
                hidden = (jax.nn.silu(gate_part) * up_projection).astype(jnp.bfloat16)
                partial_value = jnp.einsum("rqh,qhf->rqf", hidden.reshape(-1, split, HS).astype(jnp.float32), wd[lower:lower + HE].reshape(split, HS, D).astype(jnp.float32))
                summed = jnp.sum(partial_value.astype(jnp.bfloat16).astype(jnp.float32), axis=1)
                output_rows.append(summed.reshape(2, N_EXPERT, MOST, D))
            output_rows = jnp.stack(output_rows)
            mixture_weights = placement_slot * weight_matrix[..., None]
            mixture_of_experts = jnp.einsum("dnrem,ednmf->dnrf", mixture_weights, output_rows, precision=lax.Precision.HIGHEST)
            return (block.astype(jnp.float32) + mixture_of_experts).astype(jnp.bfloat16)

        packs = (jnp.moveaxis(carry_state, 1, 0), jnp.moveaxis(ids, 1, 0), jnp.moveaxis(gates, 1, 0), w_gate, w_up, w_down)
        updated = jnp.moveaxis(lax.map(one_section, packs), 0, 1)
        carry_state = jnp.stack([jnp.roll(updated[0], 1, axis=0), jnp.roll(updated[1], -1, axis=0)])
    return carry_state.reshape(2, N_SECTION * N_EXPERT * ROWS, D)
```

```python
import functools

import jax
import jax.numpy as jnp
from jax import lax
from jax.experimental import pallas as pl
from jax.experimental.pallas import tpu as pltpu
from jax.sharding import PartitionSpec as P

MOST = 6
STEPS = 2
ROWS = 64
DIRS = 2
GROUPS = 4
CHIPS = 4
CORES = 2
FOLD = 2
PART = FOLD * DIRS * MOST
PARAMS = pltpu.CompilerParams(vmem_limit_bytes=48 * 1024 * 1024)


def device_at(g, m, c):
    return (g * CHIPS + m) * CORES + c


def pairs_of(place):
    pairs = []
    for g in range(GROUPS):
        for m in range(CHIPS):
            for c in range(CORES):
                pairs.append((device_at(g, m, c), device_at(*place(g, m, c))))
    return pairs


def group_shift(value, k):
    return lax.ppermute(value, "expert", pairs_of(lambda g, m, c: ((g + k) % GROUPS, m, c)))


def chip_shift(value, k):
    return lax.ppermute(value, "expert", pairs_of(lambda g, m, c: (g, (m + k) % CHIPS, c)))


def core_swap(value):
    return lax.ppermute(value, "expert", pairs_of(lambda g, m, c: (g, m, 1 - c)))


def section_shift(value, steps):
    count = lax.axis_size("section")
    return lax.ppermute(value, "section", [(s, (s + steps) % count) for s in range(count)])


def route_tables(ids, gates, group):
    norm = gates / jnp.sum(gates, axis=-1, keepdims=True)
    names = (group + jnp.arange(GROUPS, dtype=jnp.int32)) % GROUPS
    picks = ids[..., None] == names
    member = jnp.any(picks, axis=-2).astype(jnp.int32)
    weight = jnp.sum(jnp.where(picks, norm[..., None], 0.0), axis=-2)
    rank = jnp.cumsum(member, axis=-2) - member
    slot = (rank[..., None] == jnp.arange(MOST, dtype=jnp.int32)) & (member[..., None] > 0)
    slot = slot.astype(jnp.float32)
    fold = jnp.eye(FOLD, dtype=jnp.float32)
    way = jnp.eye(DIRS, dtype=jnp.float32)
    listing = jnp.einsum("dtks,qp,de->kqdspet", slot, fold, way, precision=lax.Precision.HIGHEST)
    mixing = jnp.einsum(
        "dtks,qp,de->qdtkpes", slot * weight[..., None], fold, way, precision=lax.Precision.HIGHEST
    )
    listing = listing.reshape(GROUPS * PART, FOLD * DIRS * ROWS).astype(jnp.bfloat16)
    mixing = mixing.reshape(FOLD * DIRS * ROWS, GROUPS * PART)
    high = mixing.astype(jnp.bfloat16)
    low = (mixing - high.astype(jnp.float32)).astype(jnp.bfloat16)
    return listing, jnp.concatenate([high, low], axis=1)


def stacked(states, width):
    return jnp.concatenate(
        [state[:, q * width : (q + 1) * width] for q in range(FOLD) for state in states], axis=0
    )


def list_kernel(listing_ref, *refs):
    states = [ref[...] for ref in refs[:DIRS]]
    outs = refs[DIRS:]
    width = outs[0].shape[1]
    rows = jnp.dot(listing_ref[...], stacked(states, width), preferred_element_type=jnp.float32)
    for k, out in enumerate(outs):
        out[...] = rows[k * PART : (k + 1) * PART].astype(jnp.bfloat16)


def list_rows(listing, states):
    width = states[0].shape[1] // FOLD
    return pl.pallas_call(
        list_kernel,
        out_shape=[jax.ShapeDtypeStruct((PART, width), jnp.bfloat16)] * GROUPS,
        compiler_params=PARAMS,
    )(listing, *states)


def expert_kernel(gate_up_ref, down_ref, *refs):
    ins, outs = refs[:CHIPS], refs[CHIPS:]
    rows_each, width = ins[0].shape
    hidden_units = down_ref.shape[0]
    total = rows_each * CHIPS
    rows = jnp.concatenate([ref[...] for ref in ins], axis=0)
    place = lax.broadcasted_iota(jnp.int32, (total, 1), 0)
    piece = (place % PART) // (PART // FOLD)
    sums = jnp.zeros((total, 2 * hidden_units), jnp.float32)
    for q in range(FOLD):
        part = jnp.dot(
            rows, gate_up_ref[q * width : (q + 1) * width], preferred_element_type=jnp.float32
        )
        sums = sums + jnp.where(piece == q, part, 0.0)
    one = lax.broadcasted_iota(jnp.int32, (rows_each, rows_each), 0)
    two = lax.broadcasted_iota(jnp.int32, (rows_each, rows_each), 1)
    step = PART // FOLD
    same = ((one // PART) == (two // PART)) & ((one % step) == (two % step))
    same = same.astype(jnp.float32)
    hidden = []
    for n in range(CHIPS):
        both = jnp.dot(
            same,
            sums[n * rows_each : (n + 1) * rows_each],
            precision=lax.Precision.HIGHEST,
            preferred_element_type=jnp.float32,
        )
        gate, up = both[:, :hidden_units], both[:, hidden_units:]
        hidden.append(jax.nn.silu(gate) * up)
    hidden = jnp.concatenate(hidden, axis=0)
    result = jnp.zeros((total, width), jnp.float32)
    for q in range(FOLD):
        chosen = jnp.where(piece == q, hidden, 0.0).astype(jnp.bfloat16)
        result = result + jnp.dot(
            chosen, down_ref[:, q * width : (q + 1) * width], preferred_element_type=jnp.float32
        )
    for n, out in enumerate(outs):
        out[...] = result[n * rows_each : (n + 1) * rows_each].astype(jnp.bfloat16)


def expert_rows(gate_up, down, rows):
    return pl.pallas_call(
        expert_kernel,
        out_shape=[jax.ShapeDtypeStruct(rows[0].shape, jnp.bfloat16)] * CHIPS,
        compiler_params=PARAMS,
    )(gate_up, down, *rows)


def sum_kernel(*refs):
    ins, outs = refs[:CHIPS], refs[CHIPS:]
    total = ins[0][...].astype(jnp.float32)
    for ref in ins[1:]:
        total = total + ref[...].astype(jnp.float32)
    for k, out in enumerate(outs):
        out[...] = total[k * PART : (k + 1) * PART].astype(jnp.bfloat16)


def sum_rows(parts):
    width = parts[0].shape[1]
    return pl.pallas_call(
        sum_kernel,
        out_shape=[jax.ShapeDtypeStruct((PART, width), jnp.bfloat16)] * GROUPS,
        compiler_params=PARAMS,
    )(*parts)


def mix_kernel(mixing_ref, *refs):
    states = [ref[...] for ref in refs[:DIRS]]
    rows = [ref[...].astype(jnp.float32) for ref in refs[DIRS : DIRS + GROUPS]]
    outs = refs[DIRS + GROUPS :]
    width = rows[0].shape[1]
    rows = jnp.concatenate(rows, axis=0).astype(jnp.bfloat16)
    half = GROUPS * PART
    mixed = jnp.dot(mixing_ref[:, :half], rows, preferred_element_type=jnp.float32)
    mixed = mixed + jnp.dot(mixing_ref[:, half:], rows, preferred_element_type=jnp.float32)
    for q in range(FOLD):
        for d, out in enumerate(outs):
            start = (q * DIRS + d) * ROWS
            old = states[d][:, q * width : (q + 1) * width].astype(jnp.float32)
            out[:, q * width : (q + 1) * width] = (old + mixed[start : start + ROWS]).astype(
                jnp.bfloat16
            )


def mix_rows(mixing, states, rows):
    return pl.pallas_call(
        mix_kernel,
        out_shape=[jax.ShapeDtypeStruct(states[0].shape, jnp.bfloat16)] * DIRS,
        compiler_params=PARAMS,
    )(mixing, *states, *rows)


def body(activations, expert_ids, gate_values, w_gate, w_up, w_down):
    group = lax.axis_index("expert") // (CHIPS * CORES)
    tables = [route_tables(expert_ids[s], gate_values[s], group) for s in range(STEPS)]
    gate_up = jnp.concatenate([w_gate[0], core_swap(w_gate[0]), w_up[0], core_swap(w_up[0])], axis=1)
    down = jnp.concatenate([w_down[0], core_swap(w_down[0])], axis=0)
    states = [activations[d] for d in range(DIRS)]
    for step in range(STEPS):
        listing, mixing = tables[step]
        sent = list_rows(listing, states)
        held = jnp.concatenate(
            [group_shift(sent[k], k) if k else sent[0] for k in range(GROUPS)], axis=0
        )
        rows = [chip_shift(held, k) if k else held for k in range(CHIPS)]
        done = expert_rows(gate_up, down, rows)
        parts = [chip_shift(done[k], -k) if k else done[0] for k in range(CHIPS)]
        summed = sum_rows(parts)
        back = [group_shift(summed[k], -k) if k else summed[0] for k in range(GROUPS)]
        updated = mix_rows(mixing, states, back)
        states = [section_shift(updated[0], 1), section_shift(updated[1], -1)]
    return jnp.stack(states)


def solution(mesh):
    placed = (
        P(None, ("section", "expert"), None),
        P(None, None, ("section", "expert"), None),
        P(None, None, ("section", "expert"), None),
        P("section", None, "expert"),
        P("section", None, "expert"),
        P("section", "expert", None),
    )
    return jax.shard_map(
        body,
        mesh=mesh,
        in_specs=placed,
        out_specs=P(None, ("section", "expert"), None),
        check_vma=False,
    )
```

```python
import jax
import jax.numpy as jnp
from jax import lax
from jax.experimental import pallas as pl
from jax.experimental.pallas import tpu as pltpu
from jax.sharding import PartitionSpec as P

MOST = 6
STEPS = 2
ROWS = 64
GROUPS = 4
CHIPS = 4
CORES = 2
PIECES = 2
DIRS = 2
FOLD = 2
EACH = DIRS * MOST
PART = FOLD * EACH
LISTED = GROUPS * MOST
PARAMS = pltpu.CompilerParams(vmem_limit_bytes=52 * 1024 * 1024)


def device_at(g, m, c):
    return (g * CHIPS + m) * CORES + c


def pairs_of(place):
    pairs = []
    for g in range(GROUPS):
        for m in range(CHIPS):
            for c in range(CORES):
                pairs.append((device_at(g, m, c), device_at(*place(g, m, c))))
    return pairs


def group_exchange(value):
    groups = [
        [device_at(g, m, c) for g in range(GROUPS)] for m in range(CHIPS) for c in range(CORES)
    ]
    return lax.all_to_all(
        value, "expert", split_axis=0, concat_axis=0, axis_index_groups=groups, tiled=True
    )


def chip_swap(value, k):
    return lax.ppermute(value, "expert", pairs_of(lambda g, m, c: (g, m ^ k, c)))


def core_swap(value):
    return lax.ppermute(value, "expert", pairs_of(lambda g, m, c: (g, m, 1 - c)))


def section_shift(value, steps):
    count = lax.axis_size("section")
    return lax.ppermute(value, "section", [(s, (s + steps) % count) for s in range(count)])


def local_call(kernel, shapes, *operands):
    return pl.pallas_call(
        kernel,
        out_shape=[jax.ShapeDtypeStruct(shape, jnp.bfloat16) for shape in shapes],
        compiler_params=PARAMS,
    )(*operands)


def dot(a, b):
    return jnp.dot(a, b, preferred_element_type=jnp.float32)


def one_hot(mask):
    return mask.astype(jnp.float32).astype(jnp.bfloat16)


def listed_slots(ids):
    shape = (ROWS, GROUPS * PART)
    lane = lax.broadcasted_iota(jnp.int32, shape, 1)
    member = jnp.zeros(shape, jnp.float32)
    for e in range(GROUPS):
        named = jnp.max((ids == e).astype(jnp.float32), axis=1, keepdims=True)
        member = member + jnp.where(lane // PART == e, named, 0.0)
    later = lax.broadcasted_iota(jnp.int32, (ROWS, ROWS), 0)
    earlier = lax.broadcasted_iota(jnp.int32, (ROWS, ROWS), 1)
    rank = dot(one_hot(earlier < later), member.astype(jnp.bfloat16))
    slot = (lane % MOST).astype(jnp.float32)
    return jnp.where((rank == slot) & (member > 0.0), 1.0, 0.0)


def spread(tables):
    lane = lax.broadcasted_iota(jnp.int32, tables[0].shape, 1)
    block = (lane % PART) // MOST
    rows = [
        jnp.where(block == q * DIRS + d, tables[d], 0.0) for q in range(FOLD) for d in range(DIRS)
    ]
    return jnp.concatenate(rows, axis=0)


def fold_match(folded, plain, q, d):
    same_expert = (folded // PART) == (plain // MOST)
    same_slot = (folded % MOST) == (plain % MOST)
    this_block = ((folded % PART) // MOST) == q * DIRS + d
    return one_hot(same_expert & same_slot & this_block)


def list_kernel(ids_ref, *refs):
    states, out_ref = refs[:DIRS], refs[DIRS]
    width = out_ref.shape[1]
    table = spread([listed_slots(ids_ref[d]) for d in range(DIRS)]).astype(jnp.bfloat16)
    stack = [ref[:, q * width : (q + 1) * width] for q in range(FOLD) for ref in states]
    rows = lax.dot_general(
        table,
        jnp.concatenate(stack, axis=0),
        (((0,), (0,)), ((), ())),
        preferred_element_type=jnp.float32,
    )
    out_ref[...] = rows.astype(jnp.bfloat16)


def unfold_kernel(folded_ref, *outs):
    rows = folded_ref[...]
    width = rows.shape[1]
    shape = (LISTED, rows.shape[0])
    plain = lax.broadcasted_iota(jnp.int32, shape, 0)
    folded = lax.broadcasted_iota(jnp.int32, shape, 1)
    for d, out in enumerate(outs):
        for q in range(FOLD):
            part = dot(fold_match(folded, plain, q, d), rows)
            out[:, q * width : (q + 1) * width] = part.astype(jnp.bfloat16)


def pair_kernel(near_ref, far_ref, out_ref):
    rows = [ref[...].astype(jnp.float32) for ref in (near_ref, far_ref)]
    out_ref[...] = jnp.concatenate(rows, axis=0).astype(jnp.bfloat16)


def add_kernel(own_ref, got_ref, near_ref, far_ref):
    rows = near_ref.shape[0]
    total = own_ref[...].astype(jnp.float32) + got_ref[...].astype(jnp.float32)
    near_ref[...] = total[:rows].astype(jnp.bfloat16)
    far_ref[...] = total[rows:].astype(jnp.bfloat16)


def expert_kernel(*refs):
    pieces = refs[: 3 * PIECES]
    near_ref, far_ref, done_near_ref, done_far_ref = refs[3 * PIECES :]
    rows = jnp.concatenate([near_ref[...], far_ref[...]], axis=0)
    result = jnp.zeros(rows.shape, jnp.float32)
    for p in range(0, PIECES, 2):
        gates, ups, downs = ([ref[...] for ref in pieces[3 * p + n : 3 * p + 6 : 3]] for n in range(3))
        both = dot(rows, jnp.concatenate(gates + ups, axis=1))
        half = both.shape[1] // 2
        hidden = (jax.nn.silu(both[:, :half]) * both[:, half:]).astype(jnp.bfloat16)
        result = result + dot(hidden, jnp.concatenate(downs, axis=0))
    count = near_ref.shape[0]
    done_near_ref[...] = result[:count].astype(jnp.bfloat16)
    done_far_ref[...] = result[count:].astype(jnp.bfloat16)


def fold_kernel(*refs):
    owns, gots, out_ref = refs[:DIRS], refs[DIRS : 2 * DIRS], refs[2 * DIRS]
    width = out_ref.shape[1]
    shape = (out_ref.shape[0], LISTED)
    folded = lax.broadcasted_iota(jnp.int32, shape, 0)
    plain = lax.broadcasted_iota(jnp.int32, shape, 1)
    rows = jnp.zeros(out_ref.shape, jnp.float32)
    for d in range(DIRS):
        total = owns[d][...].astype(jnp.float32) + gots[d][...].astype(jnp.float32)
        total = total.astype(jnp.bfloat16)
        for q in range(FOLD):
            part = total[:, q * width : (q + 1) * width]
            rows = rows + dot(fold_match(folded, plain, q, d), part)
    out_ref[...] = rows.astype(jnp.bfloat16)


def weighted_slots(ids, gates):
    norm = gates / jnp.sum(gates, axis=1, keepdims=True)
    slots = listed_slots(ids)
    lane = lax.broadcasted_iota(jnp.int32, slots.shape, 1)
    weight = jnp.zeros(slots.shape, jnp.float32)
    for e in range(GROUPS):
        chosen = jnp.sum(jnp.where(ids == e, norm, 0.0), axis=1, keepdims=True)
        weight = weight + jnp.where(lane // PART == e, chosen, 0.0)
    return slots * weight


def mix_kernel(ids_ref, gates_ref, *refs):
    states, home_ref, outs = refs[:DIRS], refs[DIRS], refs[DIRS + 1 :]
    mixing = spread([weighted_slots(ids_ref[d], gates_ref[d]) for d in range(DIRS)])
    high = mixing.astype(jnp.bfloat16)
    low = (mixing - high.astype(jnp.float32)).astype(jnp.bfloat16)
    rows = home_ref[...]
    width = rows.shape[1]
    mixed = dot(high, rows) + dot(low, rows)
    for q in range(FOLD):
        for d in range(DIRS):
            at = (q * DIRS + d) * ROWS
            old = states[d][:, q * width : (q + 1) * width].astype(jnp.float32)
            outs[d][:, q * width : (q + 1) * width] = (old + mixed[at : at + ROWS]).astype(
                jnp.bfloat16
            )


def expert_step(states, ids, gates, weights):
    rows, model = states[0].shape
    width = model // FOLD
    (sent,) = local_call(list_kernel, [(GROUPS * PART, width)], ids, *states)
    held = group_exchange(sent)
    near = local_call(unfold_kernel, [(LISTED, model)] * DIRS, held)
    owns, gots = [], []
    for d in range(DIRS):
        far = chip_swap(near[d], 2)
        (pair,) = local_call(pair_kernel, [(2 * LISTED, model)], near[d], far)
        other = chip_swap(pair, 1)
        done, sent_back = local_call(
            expert_kernel, [(2 * LISTED, model)] * 2, *weights, pair, other
        )
        got = chip_swap(sent_back, 1)
        own, passed = local_call(add_kernel, [(LISTED, model)] * 2, done, got)
        owns.append(own)
        gots.append(chip_swap(passed, 2))
    (summed,) = local_call(fold_kernel, [(GROUPS * PART, width)], *owns, *gots)
    home = group_exchange(summed)
    return local_call(mix_kernel, [(rows, model)] * DIRS, ids, gates, *states, home)


def body(activations, expert_ids, gate_values, w_gate, w_up, w_down):
    own = [w_gate[0], w_up[0], w_down[0]]
    weights = own + [core_swap(value) for value in own]
    states = [activations[d] for d in range(DIRS)]
    for step in range(STEPS):
        updated = expert_step(states, expert_ids[step], gate_values[step], weights)
        states = [section_shift(updated[0], 1), section_shift(updated[1], -1)]
    return jnp.stack(states)


def solution(mesh):
    placed = (
        P(None, ("section", "expert"), None),
        P(None, None, ("section", "expert"), None),
        P(None, None, ("section", "expert"), None),
        P("section", None, "expert"),
        P("section", None, "expert"),
        P("section", "expert", None),
    )
    return jax.shard_map(
        body,
        mesh=mesh,
        in_specs=placed,
        out_specs=P(None, ("section", "expert"), None),
        check_vma=False,
    )
```

```python
import jax
import jax.numpy as jnp
from jax import lax
from jax.experimental import pallas as pl
from jax.experimental.pallas import tpu as pltpu
from jax.sharding import PartitionSpec as P

MOST = 6
STEPS = 2
ROWS = 64
GROUPS = 4
CHIPS = 4
CORES = 2
PIECES = 2
DIRS = 2
FOLD = 2
EACH = DIRS * MOST
PART = FOLD * EACH
LISTED = GROUPS * MOST
MIB = 1024 * 1024


def device_at(g, m, c):
    return (g * CHIPS + m) * CORES + c


def pairs_of(place):
    pairs = []
    for g in range(GROUPS):
        for m in range(CHIPS):
            for c in range(CORES):
                pairs.append((device_at(g, m, c), device_at(*place(g, m, c))))
    return pairs


def group_exchange(value):
    groups = [
        [device_at(g, m, c) for g in range(GROUPS)] for m in range(CHIPS) for c in range(CORES)
    ]
    return lax.all_to_all(
        value, "expert", split_axis=0, concat_axis=0, axis_index_groups=groups, tiled=True
    )


def chip_swap(value, k):
    return lax.ppermute(value, "expert", pairs_of(lambda g, m, c: (g, m ^ k, c)))


def core_swap(value):
    return lax.ppermute(value, "expert", pairs_of(lambda g, m, c: (g, m, 1 - c)))


def section_shift(value, steps):
    count = lax.axis_size("section")
    return lax.ppermute(value, "section", [(s, (s + steps) % count) for s in range(count)])


def local_call(kernel, shapes, *operands, vmem=52):
    return pl.pallas_call(
        kernel,
        out_shape=[jax.ShapeDtypeStruct(shape, jnp.bfloat16) for shape in shapes],
        compiler_params=pltpu.CompilerParams(vmem_limit_bytes=vmem * MIB),
    )(*operands)


def dot(a, b):
    return jnp.dot(a, b, preferred_element_type=jnp.float32)


def one_hot(mask):
    return mask.astype(jnp.float32).astype(jnp.bfloat16)


def listed_slots(ids, part):
    shape = (ROWS, GROUPS * part)
    lane = lax.broadcasted_iota(jnp.int32, shape, 1)
    member = jnp.zeros(shape, jnp.float32)
    for e in range(GROUPS):
        named = jnp.max((ids == e).astype(jnp.float32), axis=1, keepdims=True)
        member = member + jnp.where(lane // part == e, named, 0.0)
    later = lax.broadcasted_iota(jnp.int32, (ROWS, ROWS), 0)
    earlier = lax.broadcasted_iota(jnp.int32, (ROWS, ROWS), 1)
    rank = dot(one_hot(earlier < later), member.astype(jnp.bfloat16))
    slot = (lane % MOST).astype(jnp.float32)
    return jnp.where((rank == slot) & (member > 0.0), 1.0, 0.0)


def spread(tables):
    lane = lax.broadcasted_iota(jnp.int32, tables[0].shape, 1)
    block = (lane % PART) // MOST
    rows = [
        jnp.where(block == q * DIRS + d, tables[d], 0.0) for q in range(FOLD) for d in range(DIRS)
    ]
    return jnp.concatenate(rows, axis=0)


def fold_match(folded, plain, q, d):
    same_expert = (folded // PART) == (plain // MOST)
    same_slot = (folded % MOST) == (plain % MOST)
    this_block = ((folded % PART) // MOST) == q * DIRS + d
    return one_hot(same_expert & same_slot & this_block)


def list_kernel(ids_ref, *refs):
    states, out_ref = refs[:DIRS], refs[DIRS]
    width = out_ref.shape[1]
    table = spread([listed_slots(ids_ref[d], PART) for d in range(DIRS)]).astype(jnp.bfloat16)
    stack = [ref[:, q * width : (q + 1) * width] for q in range(FOLD) for ref in states]
    rows = lax.dot_general(
        table,
        jnp.concatenate(stack, axis=0),
        (((0,), (0,)), ((), ())),
        preferred_element_type=jnp.float32,
    )
    out_ref[...] = rows.astype(jnp.bfloat16)


def unfold_kernel(folded_ref, *outs):
    rows = folded_ref[...]
    width = rows.shape[1]
    shape = (LISTED, rows.shape[0])
    plain = lax.broadcasted_iota(jnp.int32, shape, 0)
    folded = lax.broadcasted_iota(jnp.int32, shape, 1)
    for d, out in enumerate(outs):
        for q in range(FOLD):
            part = dot(fold_match(folded, plain, q, d), rows)
            out[:, q * width : (q + 1) * width] = part.astype(jnp.bfloat16)


def pair_kernel(near_ref, far_ref, out_ref):
    rows = [ref[...].astype(jnp.float32) for ref in (near_ref, far_ref)]
    out_ref[...] = jnp.concatenate(rows, axis=0).astype(jnp.bfloat16)


def add_kernel(own_ref, got_ref, near_ref, far_ref):
    rows = near_ref.shape[0]
    total = own_ref[...].astype(jnp.float32) + got_ref[...].astype(jnp.float32)
    near_ref[...] = total[:rows].astype(jnp.bfloat16)
    far_ref[...] = total[rows:].astype(jnp.bfloat16)


def expert_kernel(*refs):
    pieces = refs[: 3 * PIECES]
    near_ref, far_ref, done_near_ref, done_far_ref = refs[3 * PIECES :]
    rows = jnp.concatenate([near_ref[...], far_ref[...]], axis=0)
    result = jnp.zeros(rows.shape, jnp.float32)
    for p in range(0, PIECES, 2):
        gates, ups, downs = ([ref[...] for ref in pieces[3 * p + n : 3 * p + 6 : 3]] for n in range(3))
        both = dot(rows, jnp.concatenate(gates + ups, axis=1))
        half = both.shape[1] // 2
        hidden = (jax.nn.silu(both[:, :half]) * both[:, half:]).astype(jnp.bfloat16)
        result = result + dot(hidden, jnp.concatenate(downs, axis=0))
    count = near_ref.shape[0]
    done_near_ref[...] = result[:count].astype(jnp.bfloat16)
    done_far_ref[...] = result[count:].astype(jnp.bfloat16)


def fold_kernel(*refs):
    owns, gots, out_ref = refs[:DIRS], refs[DIRS : 2 * DIRS], refs[2 * DIRS]
    width = out_ref.shape[1]
    shape = (out_ref.shape[0], LISTED)
    folded = lax.broadcasted_iota(jnp.int32, shape, 0)
    plain = lax.broadcasted_iota(jnp.int32, shape, 1)
    rows = jnp.zeros(out_ref.shape, jnp.float32)
    for d in range(DIRS):
        total = owns[d][...].astype(jnp.float32) + gots[d][...].astype(jnp.float32)
        total = total.astype(jnp.bfloat16)
        for q in range(FOLD):
            part = total[:, q * width : (q + 1) * width]
            rows = rows + dot(fold_match(folded, plain, q, d), part)
    out_ref[...] = rows.astype(jnp.bfloat16)


def split_kernel(home_ref, *outs):
    rows = home_ref[...]
    shape = (outs[0].shape[0], rows.shape[0])
    to = lax.broadcasted_iota(jnp.int32, shape, 0)
    at = lax.broadcasted_iota(jnp.int32, shape, 1)
    for d, out in enumerate(outs):
        same = (at // EACH == to // MOST) & (at % MOST == to % MOST) & ((at % EACH) // MOST == d)
        out[...] = dot(one_hot(same), rows).astype(jnp.bfloat16)


def weighted_slots(ids, gates, part):
    norm = gates / jnp.sum(gates, axis=1, keepdims=True)
    slots = listed_slots(ids, part)
    lane = lax.broadcasted_iota(jnp.int32, slots.shape, 1)
    weight = jnp.zeros(slots.shape, jnp.float32)
    for e in range(GROUPS):
        chosen = jnp.sum(jnp.where(ids == e, norm, 0.0), axis=1, keepdims=True)
        weight = weight + jnp.where(lane // part == e, chosen, 0.0)
    return slots * weight


def mix_kernel(step, top):
    def kernel(*refs):
        routes, states, homes = refs[:DIRS], refs[DIRS : 2 * DIRS], refs[2 * DIRS : 3 * DIRS]
        outs = refs[3 * DIRS :]
        for d in range(DIRS):
            route = routes[d][step]
            table = weighted_slots(route[:, :top], route[:, top:], FOLD * MOST)
            lane = lax.broadcasted_iota(jnp.int32, table.shape, 1)
            fold = (lane % (FOLD * MOST)) // MOST
            mixing = [jnp.where(fold == q, table, 0.0) for q in range(FOLD)]
            mixing = jnp.concatenate(mixing, axis=0)
            high = mixing.astype(jnp.bfloat16)
            low = (mixing - high.astype(jnp.float32)).astype(jnp.bfloat16)
            rows = homes[d][...]
            width = rows.shape[1]
            mixed = dot(high, rows) + dot(low, rows)
            out = outs[0].at[d] if len(outs) == 1 else outs[d]
            for q in range(FOLD):
                old = states[d][:, q * width : (q + 1) * width].astype(jnp.float32)
                new = old + mixed[q * ROWS : (q + 1) * ROWS]
                out[:, q * width : (q + 1) * width] = new.astype(jnp.bfloat16)

    return kernel


def both_ways(values):
    return [section_shift(value, 1 - 2 * d) for d, value in enumerate(values)]


def expert_step(states, ids, weights, early):
    model = states[0].shape[1]
    width = model // FOLD
    (sent,) = local_call(list_kernel, [(GROUPS * PART, width)], ids, *states)
    held, early = lax.optimization_barrier((group_exchange(sent), early))
    near = local_call(unfold_kernel, [(LISTED, model)] * DIRS, held)
    far = [chip_swap(near[d], 2) for d in range(DIRS)]
    _, states = lax.optimization_barrier((far[1], states))
    moved = both_ways(states)
    owns, gots = [], []
    for d in range(DIRS):
        (pair,) = local_call(pair_kernel, [(2 * LISTED, model)], near[d], far[d])
        other = chip_swap(pair, 1)
        done, sent_back = local_call(
            expert_kernel, [(2 * LISTED, model)] * 2, *weights, pair, other, vmem=32
        )
        got = chip_swap(sent_back, 1)
        own, passed = local_call(add_kernel, [(LISTED, model)] * 2, done, got)
        owns.append(own)
        gots.append(chip_swap(passed, 2))
    (summed,) = local_call(fold_kernel, [(GROUPS * PART, width)], *owns, *gots)
    home = group_exchange(summed)
    parts = local_call(split_kernel, [(GROUPS * PART // DIRS, width)] * DIRS, home)
    return both_ways(parts), moved, early


def body(activations, expert_ids, gate_values, w_gate, w_up, w_down):
    own = [w_gate[0], w_up[0], w_down[0]]
    weights = own + [core_swap(value) for value in own]
    states = [activations[d] for d in range(DIRS)]
    shape, top = states[0].shape, expert_ids.shape[-1]
    routes = jnp.concatenate([expert_ids.astype(jnp.float32), gate_values], axis=-1)
    routes = both_ways([routes[:, d] for d in range(DIRS)])
    for step in range(STEPS):
        rows, moved, routes = expert_step(states, expert_ids[step], weights, routes)
        outs = [shape] * DIRS if step < STEPS - 1 else [(DIRS, *shape)]
        states = local_call(mix_kernel(step, top), outs, *routes, *moved, *rows)
    return states[0]


def solution(mesh):
    placed = (
        P(None, ("section", "expert"), None),
        P(None, None, ("section", "expert"), None),
        P(None, None, ("section", "expert"), None),
        P("section", None, "expert"),
        P("section", None, "expert"),
        P("section", "expert", None),
    )
    return jax.shard_map(
        body,
        mesh=mesh,
        in_specs=placed,
        out_specs=P(None, ("section", "expert"), None),
        check_vma=False,
    )
```

```python
import jax
import jax.numpy as jnp
from jax import lax
from jax.experimental import pallas as pl
from jax.experimental.pallas import tpu as pltpu
from jax.sharding import PartitionSpec as P

MOST = 6
STEPS = 2
ROWS = 64
GROUPS = 4
CHIPS = 4
CORES = 2
PIECES = 2
SWAPS = ((2, 1), (1, 2))
DIRS = 2
FOLD = 2
EACH = DIRS * MOST
PART = FOLD * EACH
LISTED = GROUPS * MOST
MIB = 1024 * 1024


def device_at(g, m, c):
    return (g * CHIPS + m) * CORES + c


def pairs_of(place):
    pairs = []
    for g in range(GROUPS):
        for m in range(CHIPS):
            for c in range(CORES):
                pairs.append((device_at(g, m, c), device_at(*place(g, m, c))))
    return pairs


def group_exchange(value):
    groups = [
        [device_at(g, m, c) for g in range(GROUPS)] for m in range(CHIPS) for c in range(CORES)
    ]
    return lax.all_to_all(
        value, "expert", split_axis=0, concat_axis=0, axis_index_groups=groups, tiled=True
    )


def chip_swap(value, k):
    return lax.ppermute(value, "expert", pairs_of(lambda g, m, c: (g, m ^ k, c)))


def core_swap(value):
    return lax.ppermute(value, "expert", pairs_of(lambda g, m, c: (g, m, 1 - c)))


def section_shift(value, steps):
    count = lax.axis_size("section")
    return lax.ppermute(value, "section", [(s, (s + steps) % count) for s in range(count)])


def local_call(kernel, shapes, *operands, vmem=52):
    return pl.pallas_call(
        kernel,
        out_shape=[jax.ShapeDtypeStruct(shape, jnp.bfloat16) for shape in shapes],
        compiler_params=pltpu.CompilerParams(vmem_limit_bytes=vmem * MIB),
    )(*operands)


def dot(a, b):
    return jnp.dot(a, b, preferred_element_type=jnp.float32)


def one_hot(mask):
    return mask.astype(jnp.float32).astype(jnp.bfloat16)


def listed_slots(ids, part):
    shape = (ROWS, GROUPS * part)
    lane = lax.broadcasted_iota(jnp.int32, shape, 1)
    member = jnp.zeros(shape, jnp.float32)
    for e in range(GROUPS):
        named = jnp.max((ids == e).astype(jnp.float32), axis=1, keepdims=True)
        member = member + jnp.where(lane // part == e, named, 0.0)
    later = lax.broadcasted_iota(jnp.int32, (ROWS, ROWS), 0)
    earlier = lax.broadcasted_iota(jnp.int32, (ROWS, ROWS), 1)
    rank = dot(one_hot(earlier < later), member.astype(jnp.bfloat16))
    slot = (lane % MOST).astype(jnp.float32)
    return jnp.where((rank == slot) & (member > 0.0), 1.0, 0.0)


def spread(tables):
    lane = lax.broadcasted_iota(jnp.int32, tables[0].shape, 1)
    block = (lane % PART) // MOST
    rows = [
        jnp.where(block == q * DIRS + d, tables[d], 0.0) for q in range(FOLD) for d in range(DIRS)
    ]
    return jnp.concatenate(rows, axis=0)


def fold_match(folded, plain, q, d):
    same_expert = (folded // PART) == (plain // MOST)
    same_slot = (folded % MOST) == (plain % MOST)
    this_block = ((folded % PART) // MOST) == q * DIRS + d
    return one_hot(same_expert & same_slot & this_block)


def list_kernel(ids_ref, *refs):
    states, out_ref = refs[:DIRS], refs[DIRS]
    width = out_ref.shape[1]
    table = spread([listed_slots(ids_ref[d], PART) for d in range(DIRS)]).astype(jnp.bfloat16)
    stack = [ref[:, q * width : (q + 1) * width] for q in range(FOLD) for ref in states]
    rows = lax.dot_general(
        table,
        jnp.concatenate(stack, axis=0),
        (((0,), (0,)), ((), ())),
        preferred_element_type=jnp.float32,
    )
    out_ref[...] = rows.astype(jnp.bfloat16)


def unfold_kernel(folded_ref, *outs):
    rows = folded_ref[...]
    width = rows.shape[1]
    shape = (LISTED, rows.shape[0])
    plain = lax.broadcasted_iota(jnp.int32, shape, 0)
    folded = lax.broadcasted_iota(jnp.int32, shape, 1)
    for d, out in enumerate(outs):
        for q in range(FOLD):
            part = dot(fold_match(folded, plain, q, d), rows)
            out[:, q * width : (q + 1) * width] = part.astype(jnp.bfloat16)


def pair_kernel(near_ref, far_ref, out_ref):
    rows = [ref[...].astype(jnp.float32) for ref in (near_ref, far_ref)]
    out_ref[...] = jnp.concatenate(rows, axis=0).astype(jnp.bfloat16)


def add_kernel(own_ref, got_ref, near_ref, far_ref):
    rows = near_ref.shape[0]
    total = own_ref[...].astype(jnp.float32) + got_ref[...].astype(jnp.float32)
    near_ref[...] = total[:rows].astype(jnp.bfloat16)
    far_ref[...] = total[rows:].astype(jnp.bfloat16)


def expert_kernel(crossed):
    def kernel(*refs):
        pieces = refs[: 3 * PIECES]
        near_ref, far_ref, done_ref, passed_ref = refs[3 * PIECES :]
        rows = jnp.concatenate([near_ref[...], far_ref[...]], axis=0)
        gates, ups, downs = ([ref[...] for ref in pieces[n::3]] for n in range(3))
        both = dot(rows, jnp.concatenate(gates + ups, axis=1))
        half = both.shape[1] // 2
        hidden = (jax.nn.silu(both[:, :half]) * both[:, half:]).astype(jnp.bfloat16)
        result = dot(hidden, jnp.concatenate(downs, axis=0))
        parts = [result[n * LISTED : (n + 1) * LISTED] for n in range(CHIPS)]
        if crossed:
            parts = [parts[n] for n in (0, 2, 1, 3)]
        done_ref[...] = jnp.concatenate(parts[:2], axis=0).astype(jnp.bfloat16)
        passed_ref[...] = jnp.concatenate(parts[2:], axis=0).astype(jnp.bfloat16)

    return kernel


def fold_kernel(*refs):
    owns, gots, out_ref = refs[:DIRS], refs[DIRS : 2 * DIRS], refs[2 * DIRS]
    width = out_ref.shape[1]
    shape = (out_ref.shape[0], LISTED)
    folded = lax.broadcasted_iota(jnp.int32, shape, 0)
    plain = lax.broadcasted_iota(jnp.int32, shape, 1)
    rows = jnp.zeros(out_ref.shape, jnp.float32)
    for d in range(DIRS):
        total = owns[d][...].astype(jnp.float32) + gots[d][...].astype(jnp.float32)
        total = total.astype(jnp.bfloat16)
        for q in range(FOLD):
            part = total[:, q * width : (q + 1) * width]
            rows = rows + dot(fold_match(folded, plain, q, d), part)
    out_ref[...] = rows.astype(jnp.bfloat16)


def split_kernel(home_ref, *outs):
    rows = home_ref[...]
    shape = (outs[0].shape[0], rows.shape[0])
    to = lax.broadcasted_iota(jnp.int32, shape, 0)
    at = lax.broadcasted_iota(jnp.int32, shape, 1)
    for d, out in enumerate(outs):
        same = (at // EACH == to // MOST) & (at % MOST == to % MOST) & ((at % EACH) // MOST == d)
        out[...] = dot(one_hot(same), rows).astype(jnp.bfloat16)


def weighted_slots(ids, gates, part):
    norm = gates / jnp.sum(gates, axis=1, keepdims=True)
    slots = listed_slots(ids, part)
    lane = lax.broadcasted_iota(jnp.int32, slots.shape, 1)
    weight = jnp.zeros(slots.shape, jnp.float32)
    for e in range(GROUPS):
        chosen = jnp.sum(jnp.where(ids == e, norm, 0.0), axis=1, keepdims=True)
        weight = weight + jnp.where(lane // part == e, chosen, 0.0)
    return slots * weight


def mix_kernel(step, top):
    def kernel(*refs):
        routes, states, homes = refs[:DIRS], refs[DIRS : 2 * DIRS], refs[2 * DIRS : 3 * DIRS]
        outs = refs[3 * DIRS :]
        for d in range(DIRS):
            route = routes[d][step]
            table = weighted_slots(route[:, :top], route[:, top:], FOLD * MOST)
            lane = lax.broadcasted_iota(jnp.int32, table.shape, 1)
            fold = (lane % (FOLD * MOST)) // MOST
            mixing = [jnp.where(fold == q, table, 0.0) for q in range(FOLD)]
            mixing = jnp.concatenate(mixing, axis=0)
            high = mixing.astype(jnp.bfloat16)
            low = (mixing - high.astype(jnp.float32)).astype(jnp.bfloat16)
            rows = homes[d][...]
            width = rows.shape[1]
            mixed = dot(high, rows) + dot(low, rows)
            out = outs[0].at[d] if len(outs) == 1 else outs[d]
            for q in range(FOLD):
                old = states[d][:, q * width : (q + 1) * width].astype(jnp.float32)
                new = old + mixed[q * ROWS : (q + 1) * ROWS]
                out[:, q * width : (q + 1) * width] = new.astype(jnp.bfloat16)

    return kernel


def both_ways(values):
    return [section_shift(value, 1 - 2 * d) for d, value in enumerate(values)]


def expert_step(states, ids, weights, early):
    model = states[0].shape[1]
    width = model // FOLD
    (sent,) = local_call(list_kernel, [(GROUPS * PART, width)], ids, *states)
    held, early = lax.optimization_barrier((group_exchange(sent), early))
    near = local_call(unfold_kernel, [(LISTED, model)] * DIRS, held)
    far = [chip_swap(near[d], SWAPS[d][0]) for d in range(DIRS)]
    _, states = lax.optimization_barrier((far[1], states))
    moved = both_ways(states)
    owns, gots = [], []
    for d in range(DIRS):
        (pair,) = local_call(pair_kernel, [(2 * LISTED, model)], near[d], far[d])
        other = chip_swap(pair, SWAPS[d][1])
        done, sent_back = local_call(
            expert_kernel(SWAPS[d][1] == 2), [(2 * LISTED, model)] * 2, *weights, pair, other, vmem=32
        )
        got = chip_swap(sent_back, 1)
        own, passed = local_call(add_kernel, [(LISTED, model)] * 2, done, got)
        owns.append(own)
        gots.append(chip_swap(passed, 2))
    (summed,) = local_call(fold_kernel, [(GROUPS * PART, width)], *owns, *gots)
    home = group_exchange(summed)
    parts = local_call(split_kernel, [(GROUPS * PART // DIRS, width)] * DIRS, home)
    return both_ways(parts), moved, early


def body(activations, expert_ids, gate_values, w_gate, w_up, w_down):
    own = [w_gate[0], w_up[0], w_down[0]]
    weights = own + [core_swap(value) for value in own]
    states = [activations[d] for d in range(DIRS)]
    shape, top = states[0].shape, expert_ids.shape[-1]
    routes = jnp.concatenate([expert_ids.astype(jnp.float32), gate_values], axis=-1)
    routes = both_ways([routes[:, d] for d in range(DIRS)])
    for step in range(STEPS):
        rows, moved, routes = expert_step(states, expert_ids[step], weights, routes)
        outs = [shape] * DIRS if step < STEPS - 1 else [(DIRS, *shape)]
        states = local_call(mix_kernel(step, top), outs, *routes, *moved, *rows)
    return states[0]


def solution(mesh):
    placed = (
        P(None, ("section", "expert"), None),
        P(None, None, ("section", "expert"), None),
        P(None, None, ("section", "expert"), None),
        P("section", None, "expert"),
        P("section", None, "expert"),
        P("section", "expert", None),
    )
    return jax.shard_map(
        body,
        mesh=mesh,
        in_specs=placed,
        out_specs=P(None, ("section", "expert"), None),
        check_vma=False,
    )
```
